256 devices in a mesh: wide: 64 (over x, z, core), depth: 4 (over y).
Axes of the slice: x: 4, y: 4, z: 8, core: 2. Of those that a mesh axis runs over, the one named last changes fastest.
Arguments:
- amplitudes: bfloat16 [1024, 8, 1000], P('wide', 'depth'), may hold values from -6 to 6
- integrals: bfloat16 [8, 1000, 128, 1000], P('depth', None, 'wide'), may hold values from -0.1875 to 0.1875
- orbital_irrep: int32 [1000], replicated, may hold values from 0 to 7, as said below
- pair_irrep: int32 [1024], replicated, may hold values from 0 to 7
Outputs:
- ladder: bfloat16 [1024, 128, 1000], P('depth', 'wide')
The draws below stay inside these ranges and needn't reach their ends.
Inputs may be any that keep to these rules, and one draw needn't show every extreme that they name: `orbital_irrep`: D2h irrep labels; each irrep labels at most 256 virtual orbitals, and one irrep labels exactly 256. `pair_irrep`: D2h irrep labels.
All inputs are finite; a program needn't handle non-finite values.
Results may differ from the reference program's by a relative error of at most 0.013.
Values may be sent and summed in bfloat16 or wider, within the bound.
No kernel may reach another device: no remote copies, remote signals or barrier semaphores. Data moves between devices by JAX's collectives and lax.ppermute only.
A program may use at most 128 MiB of HBM per device.

```python
import jax
import jax.numpy as jnp
from jax import lax

NV = 1000
PAIRS = 1024
BMAX = 256
C_DEV = 2
AW = 128
CW = 8
N_DEPTH = 4


def draw_orbital_irrep(key, part):
    key = jax.random.fold_in(key, 11)
    key_big, key_perm = jax.random.split(key)
    largest = jax.random.randint(key_big, (), 0, 8, dtype=jnp.int32)
    position = jax.random.permutation(key_perm, NV).astype(jnp.int32)
    others = (largest + 1 + position % 7) % 8
    return jnp.where(position < BMAX, largest, others).astype(jnp.int32)


def with_ends(array, rng, least, high):
    index_at = [jax.random.randint(jax.random.fold_in(rng, axis), (), 0, length) for axis, length in enumerate(array.shape)]
    main_axis = array.shape.index(max(array.shape))
    beside = index_at[:main_axis] + [(index_at[main_axis] + 1) % array.shape[main_axis]] + index_at[main_axis + 1:]
    return array.at[tuple(index_at)].set(least).at[tuple(beside)].set(high)


def levels(key, extent, shards, least, high):
    gain, own = 1.0, jax.random.fold_in(key, 6)
    for dim, parts in shards:
        heights = jnp.exp(jax.random.uniform(jax.random.fold_in(own, dim), (parts,), jnp.float32, least / len(shards), high / len(shards)))
        gain = gain * jnp.repeat(heights, extent[dim] // parts).reshape([-1 if axis == dim else 1 for axis in range(len(extent))])
    return gain


def centred(stream_key, shape, deviation, reach, cuts=(), kind=jnp.bfloat16):
    drawn = jax.random.normal(stream_key, shape, jnp.float32) * deviation
    if len(cuts) > 0:
        drawn = levels(stream_key, shape, cuts, -0.22, 0.18) * drawn
    return jnp.clip(drawn, min=-reach, max=reach).astype(kind)


def setup_inputs(seed: int = 0) -> dict:
    key_of = jax.random.split(jax.random.key(seed), 5)
    amplitudes = centred(key_of[0], (PAIRS, CW, NV), 1.0, 6.0, ((0, 64), (1, 4)))
    integrals = centred(key_of[1], (CW, NV, AW, NV), (CW * NV // 8) ** -0.5, 0.1875, ((0, 4), (2, 64)))
    orbital_irrep = draw_orbital_irrep(jax.random.fold_in(key_of[4], 71), 0)
    pair_irrep = with_ends(jax.random.randint(key_of[3], (PAIRS,), 0, 8), jax.random.fold_in(key_of[3], 1), 0, 7).astype(jnp.int32)
    return dict(amplitudes=amplitudes, integrals=integrals, orbital_irrep=orbital_irrep, pair_irrep=pair_irrep)


def reference(amplitudes, integrals, orbital_irrep, pair_irrep):
    pairs = amplitudes.shape[0]
    c_labels = orbital_irrep[:CW]
    pair_left = jnp.bitwise_xor(c_labels[:, None], orbital_irrep[None, :])
    flat_amps = amplitudes.reshape(pairs, CW * NV)

    def one_orbital(orbital):
        block = lax.dynamic_index_in_dim(integrals, orbital, 2, keepdims=False)
        a_label = lax.dynamic_index_in_dim(orbital_irrep, orbital, 0, keepdims=False)
        pair_right = jnp.bitwise_xor(a_label, orbital_irrep)
        allowed = pair_left[:, :, None] == pair_right[None, None, :]
        masked = jnp.where(allowed, block, jnp.zeros((), jnp.bfloat16)).reshape(CW * NV, NV)
        total = jnp.zeros((pairs, NV), jnp.float32)
        width = C_DEV * NV
        for group in range(N_DEPTH):
            term = jnp.dot(flat_amps[:, group * width:(group + 1) * width], masked[group * width:(group + 1) * width], preferred_element_type=jnp.float32)
            rounded = lax.optimization_barrier(term.astype(jnp.bfloat16))
            total = total + rounded.astype(jnp.float32)
        out_mask = pair_irrep[:, None] == pair_right[None, :]
        return jnp.where(out_mask, total, 0.0).astype(jnp.bfloat16)

    stacked = lax.map(one_orbital, jnp.arange(AW, dtype=jnp.int32))
    return jnp.transpose(stacked, (1, 0, 2))
```

```python
import functools

import jax
import jax.numpy as jnp
from jax import lax
from jax.experimental import pallas as pl
from jax.experimental.pallas import tpu as pltpu
from jax.sharding import PartitionSpec as P

SLOTS = 256
NX, NZ, NC, NY = 4, 8, 2, 4
BF, F32, I32 = jnp.bfloat16, jnp.float32, jnp.int32
LO, HI = (0, 1, -1, 2), (-2, 3, -3, 4)
VMEM = pl.BlockSpec(memory_space=pltpu.VMEM)
ANY = pl.BlockSpec(memory_space=pl.ANY)


def coords():
    w = lax.axis_index("wide")
    return w // (NZ * NC), (w // NC) % NZ, w % NC, lax.axis_index("depth")


def pick(row, index):
    lane = lax.broadcasted_iota(I32, row.shape, 1)
    return jnp.sum(jnp.where(lane == index, row, 0), axis=1, keepdims=True)


def pack_matrix(slot):
    row = lax.broadcasted_iota(I32, (SLOTS, slot.shape[1]), 0)
    return jnp.where(row == slot, 1.0, 0.0).astype(BF)


def nt(left, right):
    return lax.dot_general(left, right, (((1,), (1,)), ((), ())), preferred_element_type=F32)


def compact_kernel(t_ref, orb_ref, pair_ref, packed_ref, slot_ref):
    x, z, core, y = coords()
    w = (x * NZ + z) * NC + core
    rows, c_count, n = t_ref.shape
    orb = orb_ref[...]
    member = jnp.where(lax.broadcasted_iota(I32, (8, n), 0) == orb, 1.0, 0.0)
    upto = jnp.where(
        lax.broadcasted_iota(I32, (128, 128), 0) <= lax.broadcasted_iota(I32, (128, 128), 1), 1.0, 0.0
    ).astype(BF)
    before = jnp.zeros((8, 1), F32)
    counts = []
    for start in range(0, n, 128):
        size = min(128, n - start)
        part = member[:, start:start + size]
        counts.append(jnp.dot(part.astype(BF), upto[:size, :size], preferred_element_type=F32) + before)
        before = before + jnp.sum(part, axis=1, keepdims=True)
    count = jnp.concatenate(counts, axis=1)
    slot = jnp.sum(member * count, axis=0, keepdims=True).astype(I32) - 1
    slot_ref[...] = slot
    onehot = pack_matrix(slot)
    pair = pair_ref[...]
    lane = lax.broadcasted_iota(I32, (rows, pair.shape[1]), 1)
    row = lax.broadcasted_iota(I32, (rows, pair.shape[1]), 0)
    pair_col = jnp.sum(jnp.where(lane == row + w * rows, pair, 0), axis=1, keepdims=True)
    amps = t_ref[...]
    for c in range(c_count):
        label = pick(orb, y * c_count + c)
        kept = jnp.where(orb == (pair_col ^ label), amps[:, c, :].astype(F32), 0.0).astype(BF)
        packed_ref[c] = nt(kept, onehot).astype(BF)


def compact(amplitudes, orb, pair):
    rows, c_count, n = amplitudes.shape
    return pl.pallas_call(
        compact_kernel,
        out_shape=(
            jax.ShapeDtypeStruct((c_count, rows, SLOTS), BF),
            jax.ShapeDtypeStruct((1, n), I32),
        ),
        in_specs=[VMEM] * 3,
        out_specs=(VMEM, VMEM),
        name="compact",
    )(amplitudes, orb, pair)


def column(row):
    return jnp.transpose(jnp.broadcast_to(row, (8, row.shape[1])))[:, :1]


def partial_kernel(offsets, a_list, add_at, final, *refs):
    n_add = len(add_at)
    blocks = refs[:16]
    v_ref, orb_ref, pair_ref, slot_ref = refs[16:20]
    adds = refs[20:20 + n_add]
    out_ref = refs[20 + n_add]
    held, spread, acc, sem = refs[21 + n_add:]
    x, z, core, y = coords()
    ai, c = pl.program_id(0), pl.program_id(1)
    n = orb_ref.shape[1]
    rows = NZ * NC * 16
    w = (x * NZ + z) * NC + core
    orb = orb_ref[...]
    dests = [lax.rem(y + off, NY) for off in offsets]

    def pair_of(dest):
        pair = pair_ref[...]
        total = jnp.zeros((1, rows), I32)
        for k in range(NY):
            total = total + jnp.where(dest == k, pair[:, rows * k:rows * (k + 1)], 0)
        return total

    pair_col = jnp.concatenate([column(pair_of(dest)) for dest in dests], axis=0)

    @pl.when((ai == 0) & (c == 0))
    def _():
        onehot = pack_matrix(slot_ref[...])
        for i, dest in enumerate(dests):
            rel = lax.rem(dest - x + NX, NX)
            for k in range(NX):
                @pl.when(rel == k)
                def _():
                    for j in range(4):
                        pltpu.make_async_copy(blocks[4 * k + j], held.at[i, j], sem.at[i, j]).start()
        for i, dest in enumerate(dests):
            for j in range(4):
                pltpu.make_async_copy(blocks[j], held.at[i, j], sem.at[i, j]).wait()
            for cc in range(2):
                parts = [None] * 16
                label = pick(orb, y * 2 + cc)
                for half, order in enumerate((LO, HI)):
                    for b, dz in enumerate(order):
                        zz = lax.rem(z + dz + NZ, NZ)
                        for other in range(NC):
                            at = zz * (NC * 16) + lax.rem(core + other, NC) * 16
                            spread[cc, pl.ds(pl.multiple_of(i * rows + at, 16), 16), :SLOTS] = held[
                                i, half * 2 + other, b, cc
                            ]
        for cc in range(2):
            label = pick(orb, y * 2 + cc)
            full = jnp.dot(spread[cc, :, :SLOTS], onehot, preferred_element_type=F32)
            spread[cc] = jnp.where(orb == (pair_col ^ label), full, 0.0).astype(BF)

    @pl.when(c == 0)
    def _():
        acc[...] = jnp.dot(spread[0], v_ref[0], preferred_element_type=F32)

    @pl.when(c == 1)
    def _():
        total = acc[...] + jnp.dot(spread[1], v_ref[0], preferred_element_type=F32)
        onehot = pack_matrix(slot_ref[...])
        for k, a in enumerate(a_list):
            @pl.when(ai == k)
            def _():
                label = pick(orb, w * 2 + a)
                kept = jnp.where(orb == (pair_col ^ label), total, 0.0).astype(BF)
                packed = nt(onehot, kept)
                for i in range(len(offsets)):
                    value = packed[:, i * rows:(i + 1) * rows]
                    for m, (off, aa) in enumerate(add_at):
                        if off == offsets[i] and aa == a:
                            value = value + adds[m][...].astype(F32)
                    if final:
                        for m, (off, aa) in enumerate(add_at):
                            if off is None and aa == a:
                                value = value + adds[m][...].astype(F32)
                        full = lax.dot_general(
                            onehot, value.astype(BF), (((0,), (0,)), ((), ())), preferred_element_type=F32
                        )
                        orb_col = column(orb)
                        keep = orb_col == (pair_of(dests[0]) ^ label)
                        out_ref[0] = jnp.where(keep, full, 0.0).astype(BF)
                    else:
                        out_ref[k * len(offsets) + i] = value.astype(BF)


def partial(blocks, v, orb, pair, slot, offsets, a_list, add_at=(), adds=(), final=False):
    n = orb.shape[1]
    rows = NZ * NC * 16
    chunk_rows = rows * len(offsets)
    if final:
        out_shape = jax.ShapeDtypeStruct((2, n, rows), BF)
        out_spec = pl.BlockSpec((1, n, rows), lambda a, c: (a, 0, 0))
    else:
        out_shape = jax.ShapeDtypeStruct((len(a_list) * len(offsets), SLOTS, rows), BF)
        out_spec = VMEM
    first = a_list[0]
    whole = lambda array: pl.BlockSpec(array.shape, lambda a, c: (0,) * array.ndim)
    flops = 2 * chunk_rows * n * n * 2 * len(a_list)
    return pl.pallas_call(
        functools.partial(partial_kernel, offsets, a_list, add_at, final),
        grid=(len(a_list), 2),
        out_shape=out_shape,
        in_specs=[ANY] * 16
        + [pl.BlockSpec((1, n, n), lambda a, c: ((a + first) * 2 + c, 0, 0))]
        + [whole(orb), whole(pair), whole(slot)]
        + [whole(add) for add in adds],
        out_specs=out_spec,
        scratch_shapes=[
            pltpu.VMEM((len(offsets), 4, 4, 2, 16, SLOTS), BF),
            pltpu.VMEM((2, chunk_rows, n), BF),
            pltpu.VMEM((chunk_rows, n), F32),
            pltpu.SemaphoreType.DMA((len(offsets), 4)),
        ],
        compiler_params=pltpu.CompilerParams(vmem_limit_bytes=40 << 20),
        cost_estimate=pl.CostEstimate(flops=flops, bytes_accessed=4 * n * n * len(a_list), transcendentals=0),
        name="partial",
    )(*blocks, v, orb, pair, slot, *adds)


def wide_perm(dx, dz, dc):
    index = lambda x, z, c: (x % NX * NZ + z % NZ) * NC + c % NC
    return [
        (index(x + dx, z + dz, c + dc), index(x, z, c)) for x in range(NX) for z in range(NZ) for c in range(NC)
    ]


def from_wide(value, dx=0, dz=0, dc=0):
    return lax.ppermute(value, "wide", wide_perm(dx, dz, dc))


def to_depth(value, dy):
    return lax.ppermute(value, "depth", [(i, (i + dy) % NY) for i in range(NY)])


def gather(block):
    at = {0: block}
    for step in range(1, 5):
        at[step] = from_wide(at[step - 1], dz=1)
        if step < 4:
            at[-step] = from_wide(at[1 - step], dz=-1)
    low = jnp.stack([at[k] for k in LO])
    high = jnp.stack([at[k] for k in HI])
    lows, highs = {0: low}, {0: high}
    for dx in (1, -1):
        lows[dx] = from_wide(low, dx=dx)
        highs[dx] = from_wide(high, dx=dx)
    lows[2] = from_wide(lows[1], dx=1)
    highs[2] = from_wide(highs[-1], dx=-1)
    out = []
    for dx in (0, 1, 2, -1):
        for value in (lows[dx], highs[dx]):
            out += [value, from_wide(value, dc=1)]
    return out


def local(amplitudes, integrals, orbital_irrep, pair_irrep):
    c_count, n, a_count, _ = integrals.shape
    orb = orbital_irrep.reshape(1, n)
    pair = pair_irrep.reshape(1, pair_irrep.shape[0])
    v = jnp.transpose(integrals, (2, 0, 1, 3)).reshape(a_count * c_count, n, n)
    packed, slot = compact(amplitudes, orb, pair)
    blocks = gather(packed)
    call = functools.partial(partial, blocks, v, orb, pair, slot)
    far = call((2,), (0, 1))
    far_up = to_depth(far[0], 1)
    far_down = to_depth(far[1], -1)
    mid0 = call((1, 3), (0,), ((1, 0),), (far_up,))
    up0, down0 = to_depth(mid0[0], 1), to_depth(mid0[1], -1)
    mid1 = call((1, 3), (1,), ((3, 1),), (far_down,))
    up1, down1 = to_depth(mid1[0], 1), to_depth(mid1[1], -1)
    out = call(
        (0,), (0, 1), ((None, 0), (None, 0), (None, 1), (None, 1)), (up0, down0, up1, down1), final=True
    )
    return jnp.transpose(out, (2, 0, 1))


def solution(mesh):
    placed = (P("wide", "depth", None), P("depth", None, "wide", None), P(), P())
    return jax.shard_map(
        local, mesh=mesh, in_specs=placed, out_specs=P("depth", "wide", None), check_vma=False
    )
```

```python
import functools

import jax
import jax.numpy as jnp
from jax import lax
from jax.experimental import pallas as pl
from jax.experimental.pallas import tpu as pltpu
from jax.sharding import PartitionSpec as P

SLOTS = 256
NX, NZ, NC, NY = 4, 8, 2, 4
ROWS = 16
CHUNK = NZ * NC * ROWS
BF, F32, I32 = jnp.bfloat16, jnp.float32, jnp.int32
VMEM = pl.BlockSpec(memory_space=pltpu.VMEM)
ANY = pl.BlockSpec(memory_space=pl.ANY)
SMALL = pltpu.CompilerParams(vmem_limit_bytes=8 << 20)
LARGE = pltpu.CompilerParams(vmem_limit_bytes=20 << 20)


def coords():
    w = lax.axis_index("wide")
    return w // (NZ * NC), (w // NC) % NZ, w % NC, lax.axis_index("depth")


def pick(row, index):
    lane = lax.broadcasted_iota(I32, row.shape, 1)
    return jnp.sum(jnp.where(lane == index, row, 0), axis=1, keepdims=True)


def pack_matrix(slot):
    row = lax.broadcasted_iota(I32, (SLOTS, slot.shape[1]), 0)
    return jnp.where(row == slot, 1.0, 0.0).astype(BF)


def column(row):
    return jnp.transpose(jnp.broadcast_to(row, (8, row.shape[1])))[:, :1]


def dot(left, right, on_left=1, on_right=0):
    return lax.dot_general(
        left, right, (((on_left,), (on_right,)), ((), ())), preferred_element_type=F32
    )


def compact_kernel(t_hbm, orb_hbm, pair_hbm, packed_ref, slot_ref, t_ref, orb_ref, pair_ref, sem):
    copies = [
        pltpu.make_async_copy(source, target, sem.at[i])
        for i, (source, target) in enumerate(((orb_hbm, orb_ref), (pair_hbm, pair_ref), (t_hbm, t_ref)))
    ]
    for copy in copies:
        copy.start()
    for copy in copies:
        copy.wait()
    x, z, core, y = coords()
    w = (x * NZ + z) * NC + core
    rows, c_count, n = t_ref.shape
    orb = orb_ref[...]
    member = jnp.where(lax.broadcasted_iota(I32, (8, n), 0) == orb, 1.0, 0.0)
    upto = jnp.where(
        lax.broadcasted_iota(I32, (128, 128), 0) <= lax.broadcasted_iota(I32, (128, 128), 1), 1.0, 0.0
    ).astype(BF)
    before = jnp.zeros((8, 1), F32)
    counts = []
    for start in range(0, n, 128):
        size = min(128, n - start)
        part = member[:, start:start + size]
        counts.append(dot(part.astype(BF), upto[:size, :size]) + before)
        before = before + jnp.sum(part, axis=1, keepdims=True)
    count = jnp.concatenate(counts, axis=1)
    slot = jnp.sum(member * count, axis=0, keepdims=True).astype(I32) - 1
    slot_ref[...] = slot
    onehot = pack_matrix(slot)
    pair = pair_ref[...]
    lane = lax.broadcasted_iota(I32, (rows, pair.shape[1]), 1)
    row = lax.broadcasted_iota(I32, (rows, pair.shape[1]), 0)
    pair_col = jnp.sum(jnp.where(lane == row + w * rows, pair, 0), axis=1, keepdims=True)
    amps = t_ref[...]
    for c in range(c_count):
        label = pick(orb, y * c_count + c)
        kept = jnp.where(orb == (pair_col ^ label), amps[:, c, :].astype(F32), 0.0).astype(BF)
        packed_ref[c] = dot(kept, onehot, 1, 1).astype(BF)


def compact(amplitudes, orb, pair):
    rows, c_count, n = amplitudes.shape
    return pl.pallas_call(
        compact_kernel,
        out_shape=(
            jax.ShapeDtypeStruct((c_count, rows, SLOTS), BF),
            jax.ShapeDtypeStruct((1, n), I32),
        ),
        in_specs=[pl.BlockSpec(memory_space=pltpu.HBM)] * 3,
        out_specs=(VMEM, VMEM),
        scratch_shapes=[
            pltpu.VMEM(amplitudes.shape, BF),
            pltpu.VMEM(orb.shape, I32),
            pltpu.VMEM(pair.shape, I32),
            pltpu.SemaphoreType.DMA((3,)),
        ],
        compiler_params=SMALL,
        name="compact",
    )(amplitudes, orb, pair)


def tables_kernel(orb_ref, slot_ref, _, pack_ref, unpack_ref, orb_col_ref):
    n = orb_ref.shape[1]
    slot = slot_ref[...]
    pack_ref[...] = pack_matrix(slot)
    lane = lax.broadcasted_iota(I32, (n, SLOTS), 1)
    unpack_ref[...] = jnp.where(lane == column(slot), 1.0, 0.0).astype(BF)
    orb_col_ref[...] = jnp.broadcast_to(column(orb_ref[...]), (n, 128))


def tables(orb, slot, after):
    n = orb.shape[1]
    return pl.pallas_call(
        tables_kernel,
        out_shape=(
            jax.ShapeDtypeStruct((SLOTS, n), BF),
            jax.ShapeDtypeStruct((n, SLOTS), BF),
            jax.ShapeDtypeStruct((n, 128), I32),
        ),
        in_specs=[VMEM] * 2 + [ANY],
        out_specs=(VMEM,) * 3,
        compiler_params=SMALL,
        name="tables",
    )(orb, slot, after)


def pair_of(pair_ref, dest):
    total = jnp.zeros((1, CHUNK), I32)
    for k in range(NY):
        total = total + jnp.where(dest == k, pair_ref[:, CHUNK * k:CHUNK * (k + 1)], 0)
    return total


def keep_matrix(orb_col_ref, label, pair_row):
    wanted = pair_row ^ label
    orb_col = orb_col_ref[...]
    return jnp.concatenate(
        [orb_col == wanted[:, at:at + 128] for at in range(0, CHUNK, 128)], axis=1
    )


def partial_kernel(offsets, *refs):
    held, v_ref = refs[:4], refs[4]
    orb_ref, pair_ref, pack_ref, unpack_ref = refs[5:9]
    out_refs, (rows_ref,) = refs[9:-1], refs[-1:]
    x, z, core, y = coords()
    w = (x * NZ + z) * NC + core
    orb = orb_ref[...]
    for i, off in enumerate(offsets):
        dest = lax.rem(y + off, NY)
        rel = x ^ dest
        for other in range(NC):
            near, late = held[2 * other:2 * other + 2]
            source = core ^ other
            first = 1 + 2 * source
            is_late = (rel != 0) & (rel != first)
            index = jnp.where(rel == first, 1, jnp.where(rel == 2, 1, 0))
            for j in range(NZ):
                zz = z ^ (7 * (j & 1)) ^ (2 * (j >> 1 & 1)) ^ (j >> 2 & 1)
                at = pl.multiple_of((zz * NC + source) * ROWS, ROWS)
                for c in range(2):
                    value = jnp.where(is_late, late[index, j, c], near[index, j, c])
                    rows_ref[i, c, pl.ds(at, ROWS), :] = value
        pair_col = jnp.broadcast_to(column(pair_of(pair_ref, dest)), (CHUNK, orb.shape[1]))
        spread = []
        for c in range(2):
            full = dot(rows_ref[i, c], pack_ref[...])
            keep = orb == (pair_col ^ pick(orb, y * 2 + c))
            spread.append(jnp.where(keep, full, 0.0).astype(BF))
        for a in range(2):
            total = dot(spread[0], v_ref[a, 0]) + dot(spread[1], v_ref[a, 1])
            keep = orb == (pair_col ^ pick(orb, w * 2 + a))
            kept = jnp.where(keep, total, 0.0).astype(BF)
            packed = dot(kept, unpack_ref[...]).astype(BF)
            out_refs[i][a] = packed


def partial(held, v, orb, pair, table, offsets):
    n = orb.shape[1]
    out_shape = [jax.ShapeDtypeStruct((2, CHUNK, SLOTS), BF)] * len(offsets)
    return pl.pallas_call(
        functools.partial(partial_kernel, offsets),
        out_shape=out_shape,
        in_specs=[VMEM] * 9,
        out_specs=[VMEM] * len(out_shape),
        scratch_shapes=[pltpu.VMEM((len(offsets), 2, CHUNK, SLOTS), BF)],
        compiler_params=LARGE,
        cost_estimate=pl.CostEstimate(
            flops=8 * CHUNK * n * n * len(offsets), bytes_accessed=8 * n * n, transcendentals=0
        ),
        name="partial",
    )(*held, v, orb, pair, *table[:2])


def join_kernel(up_ref, down_ref, far_ref, up_out, down_out):
    upward = lax.axis_index("wide") % NC == 0

    @pl.when(upward)
    def _():
        up_out[...] = (up_ref[...].astype(F32) + far_ref[...].astype(F32)).astype(BF)
        down_out[...] = down_ref[...]

    @pl.when(jnp.logical_not(upward))
    def _():
        up_out[...] = up_ref[...]
        down_out[...] = (down_ref[...].astype(F32) + far_ref[...].astype(F32)).astype(BF)


def join(up, down, far):
    return pl.pallas_call(
        join_kernel,
        out_shape=[jax.ShapeDtypeStruct(up.shape, BF)] * 2,
        in_specs=[VMEM] * 3,
        out_specs=[VMEM] * 2,
        compiler_params=SMALL,
        name="join",
    )(up, down, far)


def finish_kernel(own_ref, up_ref, down_ref, orb_ref, pair_ref, unpack_ref, orb_col_ref, out_ref):
    x, z, core, y = coords()
    w = (x * NZ + z) * NC + core
    pair_row = pair_of(pair_ref, y)
    orb = orb_ref[...]
    for a in range(2):
        total = own_ref[a].astype(F32) + up_ref[a].astype(F32) + down_ref[a].astype(F32)
        full = dot(unpack_ref[...], total.astype(BF), 1, 1)
        keep = keep_matrix(orb_col_ref, pick(orb, w * 2 + a), pair_row)
        out_ref[a] = jnp.where(keep, full, 0.0).astype(BF)


def finish(own, up, down, orb, pair, table):
    n = orb.shape[1]
    return pl.pallas_call(
        finish_kernel,
        out_shape=jax.ShapeDtypeStruct((2, n, CHUNK), BF),
        in_specs=[VMEM] * 7,
        out_specs=VMEM,
        compiler_params=SMALL,
        name="finish",
    )(own, up, down, orb, pair, *table[1:])


def swap(value, partner):
    index = lambda x, z, c: (x * NZ + z) * NC + c
    return lax.ppermute(
        value,
        "wide",
        [
            (index(x, z, c), index(*partner(x, z, c)))
            for x in range(NX) for z in range(NZ) for c in range(NC)
        ],
    )


def to_depth(value, dy_of_core):
    width = NX * NZ * NC
    return lax.ppermute(
        value,
        ("wide", "depth"),
        [(w * NY + y, w * NY + (y + dy_of_core[w % NC]) % NY) for w in range(width) for y in range(NY)],
    )


def tie_kernel(*refs):
    pass


def tie(values, *others):
    count = len(values)
    return pl.pallas_call(
        tie_kernel,
        out_shape=[jax.ShapeDtypeStruct(value.shape, value.dtype) for value in values],
        in_specs=[ANY] * (count + len(others)),
        out_specs=[ANY] * count,
        input_output_aliases={i: i for i in range(count)},
        compiler_params=SMALL,
        name="tie",
    )(*values, *others)


def gather(block, beside):
    other = lambda x, z, c: (x, z, 1 - c)
    block = block[None]
    for bit in (7, 2, 1):
        block = jnp.concatenate([block, swap(block, lambda x, z, c: (x, z ^ bit, c))])
    near = jnp.stack([block, swap(block, lambda x, z, c: (x ^ (1 + 2 * c), z, c))])
    late = swap(near, lambda x, z, c: (x ^ (3 - 2 * c), z, c))
    near_other = swap(near, other)
    (late,) = tie([late], *beside)
    return near, late, near_other, swap(late, other)


def local(amplitudes, integrals, orbital_irrep, pair_irrep):
    n = integrals.shape[1]
    orb = orbital_irrep.reshape(1, n)
    pair = pair_irrep.reshape(1, pair_irrep.shape[0])
    v = jnp.transpose(integrals, (2, 0, 1, 3))
    packed, slot = compact(amplitudes, orb, pair)
    table = tables(orb, slot, v)
    held = gather(packed, table)
    call = functools.partial(partial, held, v, orb, pair, table)
    (far,) = call((2,))
    far = to_depth(far, (1, -1))
    up, down = call((1, 3))
    up, down = join(up, down, far)
    up, down = to_depth(up, (1, 1)), to_depth(down, (-1, -1))
    (own,) = call((0,))
    out = finish(own, up, down, orb, pair, table)
    return jnp.transpose(out, (2, 0, 1))


def solution(mesh):
    placed = (P("wide", "depth", None), P("depth", None, "wide", None), P(), P())
    return jax.shard_map(
        local, mesh=mesh, in_specs=placed, out_specs=P("depth", "wide", None), check_vma=False
    )
```

```python
import functools

import jax
import jax.numpy as jnp
from jax import lax
from jax.experimental import pallas as pl
from jax.experimental.pallas import tpu as pltpu
from jax.sharding import PartitionSpec as P

SLOTS = 256
NX, NZ, NC, NY = 4, 8, 2, 4
BLOCK, HALF = 128, 512
ROWS = 16
CHUNK = NZ * NC * ROWS
PAIRS = NX * CHUNK
BF, F32, I32 = jnp.bfloat16, jnp.float32, jnp.int32
VMEM = pl.BlockSpec(memory_space=pltpu.VMEM)
ANY = pl.BlockSpec(memory_space=pl.ANY)
SMALL = pltpu.CompilerParams(vmem_limit_bytes=8 << 20)
HELD = pltpu.CompilerParams(vmem_limit_bytes=50 << 20)
LARGE = pltpu.CompilerParams(vmem_limit_bytes=20 << 20)


def coords():
    w = lax.axis_index("wide")
    return w // (NZ * NC), (w // NC) % NZ, w % NC, lax.axis_index("depth")


def pick(row, index):
    lane = lax.broadcasted_iota(I32, row.shape, 1)
    return jnp.sum(jnp.where(lane == index, row, 0), axis=1, keepdims=True)


def pack_matrix(slot):
    row = lax.broadcasted_iota(I32, (SLOTS, slot.shape[1]), 0)
    return jnp.where(row == slot, 1.0, 0.0).astype(BF)


def orb_of(labels_ref):
    return labels_ref[:, PAIRS:]


def column(row):
    return jnp.transpose(jnp.broadcast_to(row, (8, row.shape[1])))[:, :1]


def dot(left, right, on_left=1, on_right=0):
    return lax.dot_general(
        left, right, (((on_left,), (on_right,)), ((), ())), preferred_element_type=F32
    )


def compact_kernel(t_ref, labels_ref, packed_ref, slot_ref):
    x, z, core, y = coords()
    w = (x * NZ + z) * NC + core
    rows, c_count, n = t_ref.shape
    orb = orb_of(labels_ref)
    member = jnp.where(lax.broadcasted_iota(I32, (8, n), 0) == orb, 1.0, 0.0)
    upto = jnp.where(
        lax.broadcasted_iota(I32, (128, 128), 0) <= lax.broadcasted_iota(I32, (128, 128), 1), 1.0, 0.0
    ).astype(BF)
    before = jnp.zeros((8, 1), F32)
    counts = []
    for start in range(0, n, 128):
        size = min(128, n - start)
        part = member[:, start:start + size]
        counts.append(dot(part.astype(BF), upto[:size, :size]) + before)
        before = before + jnp.sum(part, axis=1, keepdims=True)
    count = jnp.concatenate(counts, axis=1)
    slot = jnp.sum(member * count, axis=0, keepdims=True).astype(I32) - 1
    slot_ref[...] = slot
    onehot = pack_matrix(slot)
    pair = labels_ref[:, :PAIRS]
    lane = lax.broadcasted_iota(I32, (rows, pair.shape[1]), 1)
    row = lax.broadcasted_iota(I32, (rows, pair.shape[1]), 0)
    pair_col = jnp.sum(jnp.where(lane == row + w * rows, pair, 0), axis=1, keepdims=True)
    amps = t_ref[...]
    for c in range(c_count):
        label = pick(orb, y * c_count + c)
        kept = jnp.where(orb == (pair_col ^ label), amps[:, c, :].astype(F32), 0.0).astype(BF)
        packed_ref[c] = dot(kept, onehot, 1, 1).astype(BF)


def compact(amplitudes, labels):
    rows, c_count, n = amplitudes.shape
    return pl.pallas_call(
        compact_kernel,
        out_shape=(
            jax.ShapeDtypeStruct((c_count, rows, SLOTS), BF),
            jax.ShapeDtypeStruct((1, n), I32),
        ),
        in_specs=[VMEM] * 2,
        out_specs=(VMEM, VMEM),
        compiler_params=SMALL,
        name="compact",
    )(amplitudes, labels)


def unweave_kernel(c, start, v_hbm, out_ref, held, sem):
    _, rows, n = out_ref.shape
    sizes = [min(BLOCK, rows - at) for at in range(0, rows, BLOCK)]
    copies = [
        pltpu.make_async_copy(
            v_hbm.at[c, pl.ds(start + k * BLOCK, size)], held.at[pl.ds(k * BLOCK, size)], sem.at[k]
        )
        for k, size in enumerate(sizes)
    ]
    for copy in copies:
        copy.start()
    for k, (size, copy) in enumerate(zip(sizes, copies)):
        to = lax.broadcasted_iota(I32, (2 * size, 2 * size), 0)
        of = lax.broadcasted_iota(I32, (2 * size, 2 * size), 1)
        order = jnp.where(of == jnp.where(to < size, 2 * to, 2 * (to - size) + 1), 1.0, 0.0).astype(BF)
        copy.wait()
        at = k * BLOCK
        both = dot(order, held[at:at + size].reshape(2 * size, n)).astype(BF)
        out_ref[0, at:at + size] = both[:size]
        out_ref[1, at:at + size] = both[size:]


def unweave(v, c, start, rows):
    _, _, a_count, n = v.shape
    return pl.pallas_call(
        functools.partial(unweave_kernel, c, start),
        out_shape=jax.ShapeDtypeStruct((a_count, rows, n), BF),
        in_specs=[ANY],
        out_specs=VMEM,
        scratch_shapes=[
            pltpu.VMEM((rows, a_count, n), BF),
            pltpu.SemaphoreType.DMA((-(-rows // BLOCK),)),
        ],
        compiler_params=HELD,
        cost_estimate=pl.CostEstimate(
            flops=8 * BLOCK * rows * n, bytes_accessed=8 * rows * n, transcendentals=0
        ),
        name="unweave",
    )(v)


def tables_kernel(labels_ref, slot_ref, pack_ref, unpack_ref, orb_col_ref):
    n = slot_ref.shape[1]
    slot = slot_ref[...]
    pack_ref[...] = pack_matrix(slot)
    lane = lax.broadcasted_iota(I32, (n, SLOTS), 1)
    unpack_ref[...] = jnp.where(lane == column(slot), 1.0, 0.0).astype(BF)
    orb_col_ref[...] = jnp.broadcast_to(column(orb_of(labels_ref)), (n, 128))


def tables(labels, slot):
    n = slot.shape[1]
    return pl.pallas_call(
        tables_kernel,
        out_shape=(
            jax.ShapeDtypeStruct((SLOTS, n), BF),
            jax.ShapeDtypeStruct((n, SLOTS), BF),
            jax.ShapeDtypeStruct((n, 128), I32),
        ),
        in_specs=[VMEM] * 2,
        out_specs=(VMEM,) * 3,
        compiler_params=SMALL,
        name="tables",
    )(labels, slot)


def pair_of(labels_ref, dest):
    total = jnp.zeros((1, CHUNK), I32)
    for k in range(NY):
        total = total + jnp.where(dest == k, labels_ref[:, CHUNK * k:CHUNK * (k + 1)], 0)
    return total


def keep_matrix(orb_col_ref, label, pair_row):
    wanted = pair_row ^ label
    orb_col = orb_col_ref[...]
    return jnp.concatenate(
        [orb_col == wanted[:, at:at + 128] for at in range(0, CHUNK, 128)], axis=1
    )


def partial_kernel(turn, *refs):
    held, v_refs = refs[:4], refs[4:8]
    labels_ref, pack_ref, unpack_ref, out_ref, rows_ref = refs[8:]
    x, z, core, y = coords()
    w = (x * NZ + z) * NC + core
    orb = orb_of(labels_ref)
    dest = y ^ jnp.where(core == 0, *turn)
    rel = x ^ dest
    index = jnp.where(rel == 3, 2, jnp.where(rel == 1, 1, 0))
    for other in range(NC):
        near, last = held[2 * other:2 * other + 2]
        source = core ^ other
        for j in range(NZ):
            zz = z ^ (7 * (j & 1)) ^ (2 * (j >> 1 & 1)) ^ (j >> 2)
            at = pl.multiple_of((zz * NC + source) * ROWS, ROWS)
            for c in range(2):
                rows_ref[c, pl.ds(at, ROWS), :] = jnp.where(rel == 2, last[j, c], near[index, j, c])
    pair_col = jnp.broadcast_to(column(pair_of(labels_ref, dest)), (CHUNK, orb.shape[1]))
    spread = []
    for c in range(2):
        full = dot(rows_ref[c], pack_ref[...])
        keep = orb == (pair_col ^ pick(orb, y * 2 + c))
        kept = jnp.where(keep, full, 0.0).astype(BF)
        spread += [kept[:, :HALF], kept[:, HALF:]]
    for a in range(2):
        total = sum(dot(left, v_ref[a]) for left, v_ref in zip(spread, v_refs))
        keep = orb == (pair_col ^ pick(orb, w * 2 + a))
        kept = jnp.where(keep, total, 0.0).astype(BF)
        out_ref[a] = dot(kept, unpack_ref[...]).astype(BF)


def partial(held, v, labels, table, turn):
    n = table[0].shape[1]
    return pl.pallas_call(
        functools.partial(partial_kernel, turn),
        out_shape=jax.ShapeDtypeStruct((2, CHUNK, SLOTS), BF),
        in_specs=[VMEM] * 11,
        out_specs=VMEM,
        scratch_shapes=[pltpu.VMEM((2, CHUNK, SLOTS), BF)],
        compiler_params=LARGE,
        cost_estimate=pl.CostEstimate(flops=8 * CHUNK * n * n, bytes_accessed=8 * n * n, transcendentals=0),
        name="partial",
    )(*held, *v, labels, *table[:2])


def add_kernel(left_ref, right_ref, out_ref):
    out_ref[...] = (left_ref[...].astype(F32) + right_ref[...].astype(F32)).astype(BF)


def add(left, right):
    return pl.pallas_call(
        add_kernel,
        out_shape=jax.ShapeDtypeStruct(left.shape, BF),
        in_specs=[VMEM] * 2,
        out_specs=VMEM,
        compiler_params=SMALL,
        name="add",
    )(left, right)


def finish_kernel(*refs):
    part_refs, (labels_ref, unpack_ref, orb_col_ref, out_ref, held, sem) = refs[:3], refs[3:]
    x, z, core, y = coords()
    w = (x * NZ + z) * NC + core
    pair_row = pair_of(labels_ref, y)
    orb = orb_of(labels_ref)
    n = orb.shape[1]
    cuts = [(a, pl.ds(at, min(HALF, n - at))) for a in range(2) for at in (0, HALF)]
    copies = [
        pltpu.make_async_copy(held.at[a, cut], out_ref.at[a, cut], sem.at[k]) for k, (a, cut) in enumerate(cuts)
    ]
    for a in range(2):
        total = sum(part_ref[a].astype(F32) for part_ref in part_refs)
        total = total.astype(BF)
        keep = keep_matrix(orb_col_ref, pick(orb, w * 2 + a), pair_row)
        for k, (of, cut) in enumerate(cuts):
            if of == a:
                full = dot(unpack_ref[cut, :], total, 1, 1)
                held[a, cut, :] = jnp.where(keep[cut.start:cut.start + cut.size], full, 0.0).astype(BF)
                copies[k].start()
    for copy in copies:
        copy.wait()


def finish(parts, labels, table):
    shape = (2, table[0].shape[1], CHUNK)
    return pl.pallas_call(
        finish_kernel,
        out_shape=jax.ShapeDtypeStruct(shape, BF),
        in_specs=[VMEM] * 6,
        out_specs=ANY,
        scratch_shapes=[pltpu.VMEM(shape, BF), pltpu.SemaphoreType.DMA((4,))],
        compiler_params=SMALL,
        name="finish",
    )(*parts, labels, *table[1:])


def swap(value, partner):
    index = lambda x, z, c: (x * NZ + z) * NC + c
    return lax.ppermute(
        value,
        "wide",
        [
            (index(x, z, c), index(*partner(x, z, c)))
            for x in range(NX) for z in range(NZ) for c in range(NC)
        ],
    )


def to_depth(value, turn):
    return lax.ppermute(
        value,
        ("wide", "depth"),
        [(w * NY + y, w * NY + (y ^ turn[w % NC])) for w in range(NX * NZ * NC) for y in range(NY)],
    )


def tie_kernel(*refs):
    pass


def tie(values, *others):
    count = len(values)
    return pl.pallas_call(
        tie_kernel,
        out_shape=[jax.ShapeDtypeStruct(value.shape, value.dtype) for value in values],
        in_specs=[ANY] * (count + len(others)),
        out_specs=[ANY] * count,
        input_output_aliases={i: i for i in range(count)},
        compiler_params=SMALL,
        name="tie",
    )(*values, *others)


def gather(block, beside):
    other = lambda x, z, c: (x, z, 1 - c)
    along_z = lambda value, bits: swap(value, lambda x, z, c: (x, z ^ bits, c))
    along_x = lambda value, bits: swap(value, lambda x, z, c: (x ^ bits, z, c))
    block = block[None]
    for k, bits in enumerate((7, 2, 1)):
        block = jnp.concatenate([block, *tie([along_z(block, bits)], *beside[k])])
    sent = swap(block, other)
    got = tie([along_x(block, bits) for bits in (1, 3)], *beside[3])
    last = along_x(got[0], 3)
    got_other = [swap(value, other) for value in got]
    (last,) = tie([last], *got_other, *beside[4])
    return jnp.stack([block, *got]), last, jnp.stack([sent, *got_other]), swap(last, other)


def local(amplitudes, integrals, orbital_irrep, pair_irrep):
    n = integrals.shape[1]
    labels = jnp.concatenate([pair_irrep, orbital_irrep]).reshape(1, PAIRS + n)
    v = [unweave(integrals, c, at, min(HALF, n - at)) for c in range(2) for at in (0, HALF)]
    packed, slot = compact(amplitudes, labels)
    table = tables(labels, slot)
    held = gather(packed, (table, [v[0]], [v[1]], [v[2]], [v[3]]))
    one, two = (3, 1), (1, 3)
    call = functools.partial(partial, held, v, labels, table)
    far = to_depth(call((2, 2)), one)
    direct = to_depth(call(one), one)
    summed = to_depth(add(call(two), far), two)
    out = finish([call((0, 0)), direct, summed], labels, table)
    return jnp.transpose(out, (2, 0, 1))


def solution(mesh):
    placed = (P("wide", "depth", None), P("depth", None, "wide", None), P(), P())
    return jax.shard_map(
        local, mesh=mesh, in_specs=placed, out_specs=P("depth", "wide", None), check_vma=False
    )
```

```python
import functools

import jax
import jax.numpy as jnp
from jax import lax
from jax.experimental import pallas as pl
from jax.experimental.pallas import tpu as pltpu
from jax.sharding import PartitionSpec as P

SLOTS = 256
NX, NZ, NC, NY = 4, 8, 2, 4
BLOCK, HALF = 128, 512
PIECES = ((0, 0, 512), (0, 512, 1000), (1, 0, 512), (1, 512, 1000))
ROWS = 16
CHUNK = NZ * NC * ROWS
PAIRS = NX * CHUNK
BF, F32, I32 = jnp.bfloat16, jnp.float32, jnp.int32
VMEM = pl.BlockSpec(memory_space=pltpu.VMEM)
ANY = pl.BlockSpec(memory_space=pl.ANY)
SMALL = pltpu.CompilerParams(vmem_limit_bytes=8 << 20)
HELD = pltpu.CompilerParams(vmem_limit_bytes=50 << 20)
LARGE = pltpu.CompilerParams(vmem_limit_bytes=20 << 20)


def coords():
    w = lax.axis_index("wide")
    return w // (NZ * NC), (w // NC) % NZ, w % NC, lax.axis_index("depth")


def pick(row, index):
    lane = lax.broadcasted_iota(I32, row.shape, 1)
    return jnp.sum(jnp.where(lane == index, row, 0), axis=1, keepdims=True)


def pack_matrix(slot):
    row = lax.broadcasted_iota(I32, (SLOTS, slot.shape[1]), 0)
    return jnp.where(row == slot, 1.0, 0.0).astype(BF)


def orb_of(labels_ref):
    return labels_ref[:, PAIRS:]


def column(row):
    return jnp.transpose(jnp.broadcast_to(row, (8, row.shape[1])))[:, :1]


def dot(left, right, on_left=1, on_right=0):
    return lax.dot_general(
        left, right, (((on_left,), (on_right,)), ((), ())), preferred_element_type=F32
    )


def compact_kernel(t_ref, labels_ref, packed_ref, slot_ref):
    x, z, core, y = coords()
    w = (x * NZ + z) * NC + core
    rows, c_count, n = t_ref.shape
    orb = orb_of(labels_ref)
    member = jnp.where(lax.broadcasted_iota(I32, (8, n), 0) == orb, 1.0, 0.0)
    upto = jnp.where(
        lax.broadcasted_iota(I32, (128, 128), 0) <= lax.broadcasted_iota(I32, (128, 128), 1), 1.0, 0.0
    ).astype(BF)
    before = jnp.zeros((8, 1), F32)
    counts = []
    for start in range(0, n, 128):
        size = min(128, n - start)
        part = member[:, start:start + size]
        counts.append(dot(part.astype(BF), upto[:size, :size]) + before)
        before = before + jnp.sum(part, axis=1, keepdims=True)
    count = jnp.concatenate(counts, axis=1)
    slot = jnp.sum(member * count, axis=0, keepdims=True).astype(I32) - 1
    slot_ref[...] = slot
    onehot = pack_matrix(slot)
    pair = labels_ref[:, :PAIRS]
    lane = lax.broadcasted_iota(I32, (rows, pair.shape[1]), 1)
    row = lax.broadcasted_iota(I32, (rows, pair.shape[1]), 0)
    pair_col = jnp.sum(jnp.where(lane == row + w * rows, pair, 0), axis=1, keepdims=True)
    amps = t_ref[...]
    for c in range(c_count):
        label = pick(orb, y * c_count + c)
        kept = jnp.where(orb == (pair_col ^ label), amps[:, c, :].astype(F32), 0.0).astype(BF)
        packed_ref[c] = dot(kept, onehot, 1, 1).astype(BF)


def compact(amplitudes, labels):
    rows, c_count, n = amplitudes.shape
    return pl.pallas_call(
        compact_kernel,
        out_shape=(
            jax.ShapeDtypeStruct((c_count, rows, SLOTS), BF),
            jax.ShapeDtypeStruct((1, n), I32),
        ),
        in_specs=[VMEM] * 2,
        out_specs=(VMEM, VMEM),
        compiler_params=SMALL,
        name="compact",
    )(amplitudes, labels)


def unweave_kernel(c, start, v_hbm, _, out_ref, held, sem):
    _, rows, n = out_ref.shape
    sizes = [min(BLOCK, rows - at) for at in range(0, rows, BLOCK)]
    copies = [
        pltpu.make_async_copy(
            v_hbm.at[c, pl.ds(start + k * BLOCK, size)], held.at[pl.ds(k * BLOCK, size)], sem.at[k]
        )
        for k, size in enumerate(sizes)
    ]
    for copy in copies:
        copy.start()
    for k, (size, copy) in enumerate(zip(sizes, copies)):
        to = lax.broadcasted_iota(I32, (2 * size, 2 * size), 0)
        of = lax.broadcasted_iota(I32, (2 * size, 2 * size), 1)
        order = jnp.where(of == jnp.where(to < size, 2 * to, 2 * (to - size) + 1), 1.0, 0.0).astype(BF)
        copy.wait()
        at = k * BLOCK
        both = dot(order, held[at:at + size].reshape(2 * size, n)).astype(BF)
        out_ref[0, at:at + size] = both[:size]
        out_ref[1, at:at + size] = both[size:]


def unweave(v, which, after):
    c, start, stop = PIECES[which]
    rows = stop - start
    _, _, a_count, n = v.shape
    return pl.pallas_call(
        functools.partial(unweave_kernel, c, start),
        out_shape=jax.ShapeDtypeStruct((a_count, rows, n), BF),
        in_specs=[ANY] * 2,
        out_specs=VMEM,
        scratch_shapes=[
            pltpu.VMEM((rows, a_count, n), BF),
            pltpu.SemaphoreType.DMA((-(-rows // BLOCK),)),
        ],
        compiler_params=HELD,
        cost_estimate=pl.CostEstimate(
            flops=8 * BLOCK * rows * n, bytes_accessed=8 * rows * n, transcendentals=0
        ),
        name="unweave",
    )(v, after)


def tables_kernel(labels_ref, slot_ref, pack_ref, unpack_ref, orb_col_ref):
    n = slot_ref.shape[1]
    slot = slot_ref[...]
    pack_ref[...] = pack_matrix(slot)
    lane = lax.broadcasted_iota(I32, (n, SLOTS), 1)
    unpack_ref[...] = jnp.where(lane == column(slot), 1.0, 0.0).astype(BF)
    orb_col_ref[...] = jnp.broadcast_to(column(orb_of(labels_ref)), (n, 128))


def tables(labels, slot):
    n = slot.shape[1]
    return pl.pallas_call(
        tables_kernel,
        out_shape=(
            jax.ShapeDtypeStruct((SLOTS, n), BF),
            jax.ShapeDtypeStruct((n, SLOTS), BF),
            jax.ShapeDtypeStruct((n, 128), I32),
        ),
        in_specs=[VMEM] * 2,
        out_specs=(VMEM,) * 3,
        compiler_params=SMALL,
        name="tables",
    )(labels, slot)


def pair_of(labels_ref, dest):
    total = jnp.zeros((1, CHUNK), I32)
    for k in range(NY):
        total = total + jnp.where(dest == k, labels_ref[:, CHUNK * k:CHUNK * (k + 1)], 0)
    return total


def keep_matrix(orb_col_ref, label, pair_row):
    wanted = pair_row ^ label
    orb_col = orb_col_ref[...]
    return jnp.concatenate(
        [orb_col == wanted[:, at:at + 128] for at in range(0, CHUNK, 128)], axis=1
    )


def partial_kernel(turn, *refs):
    held, v_refs = refs[:4], refs[4:8]
    labels_ref, pack_ref, unpack_ref, out_ref, rows_ref = refs[8:]
    x, z, core, y = coords()
    w = (x * NZ + z) * NC + core
    orb = orb_of(labels_ref)
    dest = y ^ jnp.where(core == 0, *turn)
    rel = x ^ dest
    index = jnp.where(rel == 3, 2, jnp.where(rel == 1, 1, 0))
    for other in range(NC):
        near, last = held[2 * other:2 * other + 2]
        source = core ^ other
        for j in range(NZ):
            zz = z ^ (7 * (j & 1)) ^ (j >> 1)
            at = pl.multiple_of((zz * NC + source) * ROWS, ROWS)
            for c in range(2):
                rows_ref[c, pl.ds(at, ROWS), :] = jnp.where(rel == 2, last[j, c], near[index, j, c])
    pair_col = jnp.broadcast_to(column(pair_of(labels_ref, dest)), (CHUNK, orb.shape[1]))
    spread = []
    for c in range(2):
        full = dot(rows_ref[c], pack_ref[...])
        keep = orb == (pair_col ^ pick(orb, y * 2 + c))
        kept = jnp.where(keep, full, 0.0).astype(BF)
        spread.append(kept)
    for a in range(2):
        total = sum(
            dot(spread[c][:, start:stop], v_ref[a]) for (c, start, stop), v_ref in zip(PIECES, v_refs)
        )
        keep = orb == (pair_col ^ pick(orb, w * 2 + a))
        kept = jnp.where(keep, total, 0.0).astype(BF)
        out_ref[a] = dot(kept, unpack_ref[...]).astype(BF)


def partial(held, v, labels, table, turn):
    n = table[0].shape[1]
    return pl.pallas_call(
        functools.partial(partial_kernel, turn),
        out_shape=jax.ShapeDtypeStruct((2, CHUNK, SLOTS), BF),
        in_specs=[VMEM] * 11,
        out_specs=VMEM,
        scratch_shapes=[pltpu.VMEM((2, CHUNK, SLOTS), BF)],
        compiler_params=LARGE,
        cost_estimate=pl.CostEstimate(flops=8 * CHUNK * n * n, bytes_accessed=8 * n * n, transcendentals=0),
        name="partial",
    )(*held, *v, labels, *table[:2])


def add_kernel(left_ref, right_ref, out_ref):
    out_ref[...] = (left_ref[...].astype(F32) + right_ref[...].astype(F32)).astype(BF)


def add(left, right):
    return pl.pallas_call(
        add_kernel,
        out_shape=jax.ShapeDtypeStruct(left.shape, BF),
        in_specs=[VMEM] * 2,
        out_specs=VMEM,
        compiler_params=SMALL,
        name="add",
    )(left, right)


def finish_kernel(*refs):
    part_refs, (labels_ref, unpack_ref, orb_col_ref, out_ref, held, sem) = refs[:3], refs[3:]
    x, z, core, y = coords()
    w = (x * NZ + z) * NC + core
    pair_row = pair_of(labels_ref, y)
    orb = orb_of(labels_ref)
    n = orb.shape[1]
    cuts = [(a, pl.ds(at, min(HALF, n - at))) for a in range(2) for at in (0, HALF)]
    copies = [
        pltpu.make_async_copy(held.at[a, cut], out_ref.at[a, cut], sem.at[k]) for k, (a, cut) in enumerate(cuts)
    ]
    for a in range(2):
        total = sum(part_ref[a].astype(F32) for part_ref in part_refs)
        total = total.astype(BF)
        keep = keep_matrix(orb_col_ref, pick(orb, w * 2 + a), pair_row)
        for k, (of, cut) in enumerate(cuts):
            if of == a:
                full = dot(unpack_ref[cut, :], total, 1, 1)
                held[a, cut, :] = jnp.where(keep[cut.start:cut.start + cut.size], full, 0.0).astype(BF)
                copies[k].start()
    for copy in copies:
        copy.wait()


def finish(parts, labels, table):
    shape = (2, table[0].shape[1], CHUNK)
    return pl.pallas_call(
        finish_kernel,
        out_shape=jax.ShapeDtypeStruct(shape, BF),
        in_specs=[VMEM] * 6,
        out_specs=ANY,
        scratch_shapes=[pltpu.VMEM(shape, BF), pltpu.SemaphoreType.DMA((4,))],
        compiler_params=SMALL,
        name="finish",
    )(*parts, labels, *table[1:])


def swap(value, partner):
    index = lambda x, z, c: (x * NZ + z) * NC + c
    return lax.ppermute(
        value,
        "wide",
        [
            (index(x, z, c), index(*partner(x, z, c)))
            for x in range(NX) for z in range(NZ) for c in range(NC)
        ],
    )


def to_depth(value, turn):
    return lax.ppermute(
        value,
        ("wide", "depth"),
        [(w * NY + y, w * NY + (y ^ turn[w % NC])) for w in range(NX * NZ * NC) for y in range(NY)],
    )


def tie_kernel(*refs):
    pass


def tie(values, *others):
    count = len(values)
    return pl.pallas_call(
        tie_kernel,
        out_shape=[jax.ShapeDtypeStruct(value.shape, value.dtype) for value in values],
        in_specs=[ANY] * (count + len(others)),
        out_specs=[ANY] * count,
        input_output_aliases={i: i for i in range(count)},
        compiler_params=SMALL,
        name="tie",
    )(*values, *others)


def gather(block, table, integrals):
    other = lambda x, z, c: (x, z, 1 - c)
    along_z = lambda value, bits: swap(value, lambda x, z, c: (x, z ^ bits, c))
    along_x = lambda value, bits: swap(value, lambda x, z, c: (x ^ bits, z, c))
    piece = functools.partial(unweave, integrals)
    block = block[None]
    block = jnp.concatenate([block, *tie([along_z(block, 7)], *table)])
    v = [piece(0, block)]
    block = jnp.concatenate([block, *tie([along_z(block, bits) for bits in (1, 2, 3)], *v)])
    v += [piece(1, block)]
    sent = swap(block, other)
    got = [*tie([along_x(block, 1)], *v[1:]), along_x(block, 3)]
    v += [piece(2, got[0]), piece(3, got[0])]
    last = along_x(got[0], 3)
    got_other = [swap(value, other) for value in got]
    (last,) = tie([last], *got_other, *v[2:])
    return [jnp.stack([block, *got]), last, jnp.stack([sent, *got_other]), swap(last, other)], v


def local(amplitudes, integrals, orbital_irrep, pair_irrep):
    n = integrals.shape[1]
    labels = jnp.concatenate([pair_irrep, orbital_irrep]).reshape(1, PAIRS + n)
    packed, slot = compact(amplitudes, labels)
    table = tables(labels, slot)
    held, v = gather(packed, table, integrals)
    one, two = (3, 1), (1, 3)
    call = functools.partial(partial, held, v, labels, table)
    far = to_depth(call((2, 2)), one)
    direct = to_depth(call(one), one)
    summed = to_depth(add(call(two), far), two)
    out = finish([call((0, 0)), direct, summed], labels, table)
    return jnp.transpose(out, (2, 0, 1))


def solution(mesh):
    placed = (P("wide", "depth", None), P("depth", None, "wide", None), P(), P())
    return jax.shard_map(
        local, mesh=mesh, in_specs=placed, out_specs=P("depth", "wide", None), check_vma=False
    )
```

```python
import functools

import jax
import jax.numpy as jnp
from jax import lax
from jax.experimental import pallas as pl
from jax.experimental.pallas import tpu as pltpu
from jax.sharding import PartitionSpec as P

SLOTS = 256
NX, NZ, NC, NY = 4, 8, 2, 4
BLOCK, HALF = 128, 512
PIECES = ((0, 0, 512), (0, 512, 1000), (1, 0, 512), (1, 512, 1000))
ROWS = 16
CHUNK = NZ * NC * ROWS
PAIRS = NX * CHUNK
BF, F32, I32 = jnp.bfloat16, jnp.float32, jnp.int32
VMEM = pl.BlockSpec(memory_space=pltpu.VMEM)
ANY = pl.BlockSpec(memory_space=pl.ANY)
SMALL = pltpu.CompilerParams(vmem_limit_bytes=8 << 20)
HELD = pltpu.CompilerParams(vmem_limit_bytes=50 << 20)
LARGE = pltpu.CompilerParams(vmem_limit_bytes=20 << 20)


def coords():
    w = lax.axis_index("wide")
    return w // (NZ * NC), (w // NC) % NZ, w % NC, lax.axis_index("depth")


def pick(row, index):
    lane = lax.broadcasted_iota(I32, row.shape, 1)
    return jnp.sum(jnp.where(lane == index, row, 0), axis=1, keepdims=True)


def pack_matrix(slot):
    row = lax.broadcasted_iota(I32, (SLOTS, slot.shape[1]), 0)
    return jnp.where(row == slot, 1.0, 0.0).astype(BF)


def orb_of(labels_ref):
    return labels_ref[:, PAIRS:]


def column(row):
    return jnp.transpose(jnp.broadcast_to(row, (8, row.shape[1])))[:, :1]


def dot(left, right, on_left=1, on_right=0):
    return lax.dot_general(
        left, right, (((on_left,), (on_right,)), ((), ())), preferred_element_type=F32
    )


def compact_kernel(t_ref, labels_ref, packed_ref, slot_ref):
    x, z, core, y = coords()
    w = (x * NZ + z) * NC + core
    rows, c_count, n = t_ref.shape
    orb = orb_of(labels_ref)
    member = jnp.where(lax.broadcasted_iota(I32, (8, n), 0) == orb, 1.0, 0.0)
    upto = jnp.where(
        lax.broadcasted_iota(I32, (128, 128), 0) <= lax.broadcasted_iota(I32, (128, 128), 1), 1.0, 0.0
    ).astype(BF)
    before = jnp.zeros((8, 1), F32)
    counts = []
    for start in range(0, n, 128):
        size = min(128, n - start)
        part = member[:, start:start + size]
        counts.append(dot(part.astype(BF), upto[:size, :size]) + before)
        before = before + jnp.sum(part, axis=1, keepdims=True)
    count = jnp.concatenate(counts, axis=1)
    slot = jnp.sum(member * count, axis=0, keepdims=True).astype(I32) - 1
    slot_ref[...] = slot
    onehot = pack_matrix(slot)
    pair = labels_ref[:, :PAIRS]
    lane = lax.broadcasted_iota(I32, (rows, pair.shape[1]), 1)
    row = lax.broadcasted_iota(I32, (rows, pair.shape[1]), 0)
    pair_col = jnp.sum(jnp.where(lane == row + w * rows, pair, 0), axis=1, keepdims=True)
    amps = t_ref[...]
    for c in range(c_count):
        label = pick(orb, y * c_count + c)
        kept = jnp.where(orb == (pair_col ^ label), amps[:, c, :].astype(F32), 0.0).astype(BF)
        packed_ref[c] = dot(kept, onehot, 1, 1).astype(BF)


def compact(amplitudes, labels):
    rows, c_count, n = amplitudes.shape
    return pl.pallas_call(
        compact_kernel,
        out_shape=(
            jax.ShapeDtypeStruct((c_count, rows, SLOTS), BF),
            jax.ShapeDtypeStruct((1, n), I32),
        ),
        in_specs=[VMEM] * 2,
        out_specs=(VMEM, VMEM),
        compiler_params=SMALL,
        name="compact",
    )(amplitudes, labels)


def unweave_kernel(c, start, v_hbm, _, out_ref, held, sem):
    _, rows, n = out_ref.shape
    sizes = [min(BLOCK, rows - at) for at in range(0, rows, BLOCK)]
    copies = [
        pltpu.make_async_copy(
            v_hbm.at[c, pl.ds(start + k * BLOCK, size)], held.at[pl.ds(k * BLOCK, size)], sem.at[k]
        )
        for k, size in enumerate(sizes)
    ]
    for copy in copies:
        copy.start()
    for k, (size, copy) in enumerate(zip(sizes, copies)):
        to = lax.broadcasted_iota(I32, (2 * size, 2 * size), 0)
        of = lax.broadcasted_iota(I32, (2 * size, 2 * size), 1)
        order = jnp.where(of == jnp.where(to < size, 2 * to, 2 * (to - size) + 1), 1.0, 0.0).astype(BF)
        copy.wait()
        at = k * BLOCK
        both = dot(order, held[at:at + size].reshape(2 * size, n)).astype(BF)
        out_ref[0, at:at + size] = both[:size]
        out_ref[1, at:at + size] = both[size:]


def unweave(v, which, after):
    c, start, stop = PIECES[which]
    rows = stop - start
    _, _, a_count, n = v.shape
    return pl.pallas_call(
        functools.partial(unweave_kernel, c, start),
        out_shape=jax.ShapeDtypeStruct((a_count, rows, n), BF),
        in_specs=[ANY] * 2,
        out_specs=VMEM,
        scratch_shapes=[
            pltpu.VMEM((rows, a_count, n), BF),
            pltpu.SemaphoreType.DMA((-(-rows // BLOCK),)),
        ],
        compiler_params=HELD,
        cost_estimate=pl.CostEstimate(
            flops=8 * BLOCK * rows * n, bytes_accessed=8 * rows * n, transcendentals=0
        ),
        name="unweave",
    )(v, after)


def tables_kernel(labels_ref, slot_ref, pack_ref, unpack_ref, orb_col_ref):
    n = slot_ref.shape[1]
    slot = slot_ref[...]
    pack_ref[...] = pack_matrix(slot)
    lane = lax.broadcasted_iota(I32, (n, SLOTS), 1)
    unpack_ref[...] = jnp.where(lane == column(slot), 1.0, 0.0).astype(BF)
    orb_col_ref[...] = jnp.broadcast_to(column(orb_of(labels_ref)), (n, 128))


def tables(labels, slot):
    n = slot.shape[1]
    return pl.pallas_call(
        tables_kernel,
        out_shape=(
            jax.ShapeDtypeStruct((SLOTS, n), BF),
            jax.ShapeDtypeStruct((n, SLOTS), BF),
            jax.ShapeDtypeStruct((n, 128), I32),
        ),
        in_specs=[VMEM] * 2,
        out_specs=(VMEM,) * 3,
        compiler_params=SMALL,
        name="tables",
    )(labels, slot)


def pair_of(labels_ref, dest):
    total = jnp.zeros((1, CHUNK), I32)
    for k in range(NY):
        total = total + jnp.where(dest == k, labels_ref[:, CHUNK * k:CHUNK * (k + 1)], 0)
    return total


def keep_matrix(orb_col_ref, label, pair_row):
    wanted = pair_row ^ label
    orb_col = orb_col_ref[...]
    return jnp.concatenate(
        [orb_col == wanted[:, at:at + 128] for at in range(0, CHUNK, 128)], axis=1
    )


def partial_kernel(turn, *refs):
    held, v_refs = refs[:4], refs[4:8]
    labels_ref, pack_ref, unpack_ref, out_ref, rows_ref = refs[8:]
    x, z, core, y = coords()
    w = (x * NZ + z) * NC + core
    orb = orb_of(labels_ref)
    dest = y ^ jnp.where(core == 0, *turn)
    rel = x ^ dest
    index = jnp.where(rel == 3, 2, jnp.where(rel == 1, 1, 0))
    for other in range(NC):
        near, last = held[2 * other:2 * other + 2]
        source = core ^ other
        for j in range(NZ):
            zz = z ^ (7 * (j & 1)) ^ (j >> 1)
            at = pl.multiple_of((zz * NC + source) * ROWS, ROWS)
            for c in range(2):
                rows_ref[c, pl.ds(at, ROWS), :] = jnp.where(rel == 2, last[j, c], near[index, j, c])
    pair_col = jnp.broadcast_to(column(pair_of(labels_ref, dest)), (CHUNK, orb.shape[1]))
    spread = []
    for c in range(2):
        full = dot(rows_ref[c], pack_ref[...])
        keep = orb == (pair_col ^ pick(orb, y * 2 + c))
        kept = jnp.where(keep, full, 0.0).astype(BF)
        spread.append(kept)
    for a in range(2):
        total = sum(
            dot(spread[c][:, start:stop], v_ref[a]) for (c, start, stop), v_ref in zip(PIECES, v_refs)
        )
        keep = orb == (pair_col ^ pick(orb, w * 2 + a))
        kept = jnp.where(keep, total, 0.0).astype(BF)
        out_ref[a] = dot(kept, unpack_ref[...]).astype(BF)


def partial(held, v, labels, table, turn):
    n = table[0].shape[1]
    return pl.pallas_call(
        functools.partial(partial_kernel, turn),
        out_shape=jax.ShapeDtypeStruct((2, CHUNK, SLOTS), BF),
        in_specs=[VMEM] * 11,
        out_specs=VMEM,
        scratch_shapes=[pltpu.VMEM((2, CHUNK, SLOTS), BF)],
        compiler_params=LARGE,
        cost_estimate=pl.CostEstimate(flops=8 * CHUNK * n * n, bytes_accessed=8 * n * n, transcendentals=0),
        name="partial",
    )(*held, *v, labels, *table[:2])


def add_kernel(left_ref, right_ref, out_ref):
    out_ref[...] = (left_ref[...].astype(F32) + right_ref[...].astype(F32)).astype(BF)


def add(left, right):
    return pl.pallas_call(
        add_kernel,
        out_shape=jax.ShapeDtypeStruct(left.shape, BF),
        in_specs=[VMEM] * 2,
        out_specs=VMEM,
        compiler_params=SMALL,
        name="add",
    )(left, right)


def finish_kernel(*refs):
    part_refs, (labels_ref, unpack_ref, orb_col_ref, out_ref, held, sem) = refs[:3], refs[3:]
    x, z, core, y = coords()
    w = (x * NZ + z) * NC + core
    pair_row = pair_of(labels_ref, y)
    orb = orb_of(labels_ref)
    n = orb.shape[1]
    cuts = [(a, pl.ds(at, min(HALF, n - at))) for a in range(2) for at in (0, HALF)]
    copies = [
        pltpu.make_async_copy(held.at[a, cut], out_ref.at[a, cut], sem.at[k]) for k, (a, cut) in enumerate(cuts)
    ]
    for a in range(2):
        total = sum(part_ref[a].astype(F32) for part_ref in part_refs)
        total = total.astype(BF)
        keep = keep_matrix(orb_col_ref, pick(orb, w * 2 + a), pair_row)
        for k, (of, cut) in enumerate(cuts):
            if of == a:
                full = dot(unpack_ref[cut, :], total, 1, 1)
                held[a, cut, :] = jnp.where(keep[cut.start:cut.start + cut.size], full, 0.0).astype(BF)
                copies[k].start()
    for copy in copies:
        copy.wait()


def finish(parts, labels, table):
    shape = (2, table[0].shape[1], CHUNK)
    return pl.pallas_call(
        finish_kernel,
        out_shape=jax.ShapeDtypeStruct(shape, BF),
        in_specs=[VMEM] * 6,
        out_specs=ANY,
        scratch_shapes=[pltpu.VMEM(shape, BF), pltpu.SemaphoreType.DMA((4,))],
        compiler_params=SMALL,
        name="finish",
    )(*parts, labels, *table[1:])


def swap(value, partner):
    index = lambda x, z, c: (x * NZ + z) * NC + c
    return lax.ppermute(
        value,
        "wide",
        [
            (index(x, z, c), index(*partner(x, z, c)))
            for x in range(NX) for z in range(NZ) for c in range(NC)
        ],
    )


def to_depth(value, turn):
    return lax.ppermute(
        value,
        ("wide", "depth"),
        [(w * NY + y, w * NY + (y ^ turn[w % NC])) for w in range(NX * NZ * NC) for y in range(NY)],
    )


def tie_kernel(*refs):
    pass


def tie(values, *others):
    count = len(values)
    return pl.pallas_call(
        tie_kernel,
        out_shape=[jax.ShapeDtypeStruct(value.shape, value.dtype) for value in values],
        in_specs=[ANY] * (count + len(others)),
        out_specs=[ANY] * count,
        input_output_aliases={i: i for i in range(count)},
        compiler_params=SMALL,
        name="tie",
    )(*values, *others)


def gather(block, table, integrals):
    other = lambda x, z, c: (x, z, 1 - c)
    along_z = lambda value, bits: swap(value, lambda x, z, c: (x, z ^ bits, c))
    along_x = lambda value, bits: swap(value, lambda x, z, c: (x ^ bits, z, c))
    piece = functools.partial(unweave, integrals)
    block = block[None]
    block = jnp.concatenate([block, *tie([along_z(block, 7)], *table)])
    v = [piece(0, block)]
    block = jnp.concatenate([block, *tie([along_z(block, bits) for bits in (1, 2, 3)], *v)])
    v += [piece(1, block)]
    sent = swap(block, other)
    got = [*tie([along_x(block, 1)], *v[1:]), along_x(block, 3)]
    v += [piece(2, got[0]), piece(3, got[0])]
    last = along_x(got[0], 3)
    got_other = [swap(value, other) for value in got]
    (last,) = tie([last], *got_other, *v[2:])
    return [jnp.stack([block, *got]), last, jnp.stack([sent, *got_other]), swap(last, other)], v


def local(amplitudes, integrals, orbital_irrep, pair_irrep):
    n = integrals.shape[1]
    labels = jnp.concatenate([pair_irrep, orbital_irrep]).reshape(1, PAIRS + n)
    packed, slot = compact(amplitudes, labels)
    table = tables(labels, slot)
    held, v = gather(packed, table, integrals)
    one, two = (1, 3), (3, 1)
    call = functools.partial(partial, held, v, labels, table)
    far = to_depth(call((2, 2)), one)
    direct = to_depth(call(one), one)
    summed = to_depth(add(call(two), far), two)
    out = finish([call((0, 0)), direct, summed], labels, table)
    return jnp.transpose(out, (2, 0, 1))


def solution(mesh):
    placed = (P("wide", "depth", None), P("depth", None, "wide", None), P(), P())
    return jax.shard_map(
        local, mesh=mesh, in_specs=placed, out_specs=P("depth", "wide", None), check_vma=False
    )
```
